256 devices in a mesh: section: 4 (over y), dp: 64 (over x, z, core).
Axes of the slice: x: 4, y: 4, z: 8, core: 2. Of those that a mesh axis runs over, the one named last changes fastest.
Arguments:
- inputs: bfloat16 [4, 2048, 2048], P(None, 'dp'), may hold values from -6 to 6
- route: int32 [4, 4, 2048, 6], P('section', None, 'dp'), may hold values from 0 to 63, as said below
- gain: bfloat16 [4, 2048], P('section'), may hold values from 0.099609375 to 1.8984375
- router: bfloat16 [4, 2048, 64], P('section'), may hold values from -0.125 to 0.125
- w_gate: bfloat16 [4, 64, 2048, 768], P('section', 'dp'), may hold values from -0.125 to 0.125
- w_up: bfloat16 [4, 64, 2048, 768], P('section', 'dp'), may hold values from -0.125 to 0.125
- w_down: bfloat16 [4, 64, 768, 2048], P('section', 'dp'), may hold values from -0.21875 to 0.21875
Outputs:
- states: bfloat16 [4, 4, 2048, 2048], P('section', None, 'dp')
The draws below stay inside these ranges and needn't reach their ends.
Inputs may be any that keep to these rules, and one draw needn't show every extreme that they name: `route`: each token names 6 different experts. Among the 32 tokens of one index of dp in one micro-batch and layer, no expert is named more than 6 times; in every micro-batch and layer one expert is named exactly 6 times by the tokens of every index of dp.
All inputs are finite; a program needn't handle non-finite values.
Results may differ from the reference program's by a relative error of at most 0.015.
Values may be sent and summed in bfloat16 or wider, within the bound.
No kernel may reach another device: no remote copies, remote signals or barrier semaphores. Data moves between devices by JAX's collectives and lax.ppermute only.
A program may use at most 128 MiB of HBM per device.

```python
import jax
import jax.numpy as jnp
from jax import lax

D = 2048
FF = 768
TOP = 6
TOK_DEV = 32
MICRO = 4
EXPERTS = 64
LAYERS = 4
TOKENS = 2048
PAIR = 6
CAP = 6
LOW = 0
N_DP = 64


def search_loads(cumul, spots):
    return jnp.searchsorted(cumul, spots, side='right').astype(jnp.int32)


def shuffle_rows(key):
    return jax.random.permutation(key, TOK_DEV).astype(jnp.int32)


def route_table(key):
    perm_key, load_key, shuffle_key = jax.random.split(key, 3)
    perm = jax.random.permutation(perm_key, EXPERTS).astype(jnp.int32)
    first = jax.random.randint(load_key, (N_DP, EXPERTS // 2), LOW, CAP + 1, dtype=jnp.int32)
    first = first.at[:, 0].set(CAP)
    loads = jnp.stack([first, PAIR - first], axis=2).reshape(N_DP, EXPERTS)
    cumul = jnp.cumsum(loads, axis=1).astype(jnp.int32)
    spots = jnp.arange(TOK_DEV * TOP, dtype=jnp.int32)
    where_pos = jax.vmap(search_loads, in_axes=(0, None))(cumul, spots)
    sequence = perm[jnp.clip(where_pos, 0, EXPERTS - 1)]
    table = sequence.reshape(N_DP, TOP, TOK_DEV).transpose(0, 2, 1)
    shuffles = jax.vmap(shuffle_rows)(jax.random.split(shuffle_key, N_DP))
    table = jnp.take_along_axis(table, shuffles[:, :, None], axis=1)
    return table.reshape(TOKENS, TOP)


def draw_route(key, part):
    keys = jax.random.split(jax.random.fold_in(key, 17), LAYERS * MICRO)
    tables = jax.vmap(route_table)(keys)
    return tables.reshape(LAYERS, MICRO, TOKENS, TOP).astype(jnp.int32)


def shard_levels(own_key, dims, cuts, smallest, top_value):
    def one(dim, blocks):
        draws = jax.random.uniform(jax.random.fold_in(jax.random.fold_in(own_key, 6), dim), (blocks,), jnp.float32, smallest / len(cuts), top_value / len(cuts))
        return jnp.repeat(jnp.exp(draws), dims[dim] // blocks).reshape((-1,) + (1,) * (len(dims) - dim - 1))

    factor_of = one(*cuts[0])
    for cut in cuts[1:]:
        factor_of = factor_of * one(*cut)
    return factor_of


def centred(rng, shape, spread, bound, cuts=(), held_as=jnp.bfloat16):
    drawn = spread * jax.random.normal(rng, shape, jnp.float32)
    if cuts:
        drawn = drawn * shard_levels(rng, shape, cuts, -0.22, 0.18)
    return jnp.clip(drawn, -bound, bound).astype(held_as)


def setup_inputs(seed: int = 0) -> dict:
    arg_keys = jax.random.split(jax.random.key(seed), 8)
    return {
        "inputs": centred(arg_keys[0], (MICRO, TOKENS, D), 1.0, 6.0, ((1, 64),)),
        "route": draw_route(jax.random.fold_in(arg_keys[7], 71), 0),
        "gain": jnp.clip(1.0 + 0.18 * jax.random.normal(arg_keys[2], (LAYERS, D), jnp.float32), 0.099609375, 1.8984375).astype(jnp.bfloat16),
        "router": centred(arg_keys[3], (LAYERS, D, EXPERTS), D ** -0.5, 0.125, ((0, 4),)),
        "w_gate": centred(arg_keys[4], (LAYERS, EXPERTS, D, FF), D ** -0.5, 0.125, ((0, 4), (1, 64))),
        "w_up": centred(arg_keys[5], (LAYERS, EXPERTS, D, FF), D ** -0.5, 0.125, ((0, 4), (1, 64))),
        "w_down": centred(arg_keys[6], (LAYERS, EXPERTS, FF, D), FF ** -0.5, 0.21875, ((0, 4), (1, 64))),
    }


EPS = 1e-06

def expert_rows(rows, gate_mat, up_mat, down_mat):
    gate_act = jnp.dot(rows, gate_mat, preferred_element_type=jnp.float32)
    up_act = jnp.dot(rows, up_mat, preferred_element_type=jnp.float32)
    hidden = (jax.nn.silu(gate_act) * up_act).astype(jnp.bfloat16)
    return jnp.dot(hidden, down_mat, preferred_element_type=jnp.float32).astype(jnp.bfloat16)

def reference(inputs, route, gain, router, w_gate, w_up, w_down):
    row_limit = N_DP * CAP
    copy_total = TOKENS * TOP
    expert_ids = jnp.arange(EXPERTS, dtype=jnp.int32)
    layer_inputs = [inputs[micro_no] for micro_no in range(MICRO)]
    stacked = []
    for layer_no in range(LAYERS):
        outputs_now = []
        for micro_no in range(MICRO):
            layer_in = layer_inputs[micro_no]
            chosen_ids = route[layer_no, micro_no].astype(jnp.int32)
            wide_state = layer_in.astype(jnp.float32)
            inv_rms = lax.rsqrt(lax.optimization_barrier(jnp.mean(wide_state * wide_state, axis=1, keepdims=True)) + EPS)
            normed = (wide_state * inv_rms * gain[layer_no].astype(jnp.float32)).astype(jnp.bfloat16)
            logits = jnp.dot(normed, router[layer_no], preferred_element_type=jnp.float32)
            scores = jax.nn.sigmoid(jnp.take_along_axis(logits, chosen_ids, axis=1))
            weights = scores / lax.optimization_barrier(jnp.sum(scores, axis=1, keepdims=True))
            flat_ids = chosen_ids.reshape(-1)
            sorted_copies = jnp.argsort(flat_ids, stable=True).astype(jnp.int32)
            counts = lax.optimization_barrier(jnp.sum((flat_ids[:, None] == expert_ids[None, :]).astype(jnp.int32), axis=0))
            starts = (jnp.cumsum(counts) - counts).astype(jnp.int32)
            spot_list = starts[:, None] + jnp.arange(row_limit, dtype=jnp.int32)[None, :]
            keep_mask = jnp.arange(row_limit, dtype=jnp.int32)[None, :] < counts[:, None]
            copy_index = sorted_copies[jnp.clip(spot_list, 0, copy_total - 1)]

            def per_expert(expert_no):
                rows = normed[copy_index[expert_no] // TOP]
                return expert_rows(rows, w_gate[layer_no][expert_no], w_up[layer_no][expert_no], w_down[layer_no][expert_no])
            expert_out = lax.map(per_expert, expert_ids)
            target = jnp.where(keep_mask, copy_index, copy_total).reshape(-1)
            copies = jnp.zeros((copy_total + 1, D), jnp.bfloat16).at[target].set(expert_out.reshape(-1, D))[:copy_total]
            mixed = jnp.einsum('tk,tkd->td', weights, copies.reshape(TOKENS, TOP, D).astype(jnp.float32))
            outputs_now.append((wide_state + mixed).astype(jnp.bfloat16))
        layer_inputs = outputs_now
        stacked.append(jnp.stack(outputs_now))
    return jnp.stack(stacked)
```

```python
import jax
import jax.numpy as jnp
from jax import lax
from jax.experimental import pallas as pl
from jax.experimental.pallas import tpu as pltpu
from jax.sharding import PartitionSpec as P

EPS = 1e-06
def mlp_kernel(x_ref, gu_ref, down_ref, out_ref, gu_buf, down_buf, act, gu_sems, down_sems):
    count, depth, _ = gu_ref.shape
    inner = down_ref.shape[1]
    ff = count * inner
    gu_copies = [
        pltpu.make_async_copy(gu_ref.at[j], gu_buf.at[j], gu_sems.at[j]) for j in range(count)
    ]
    down_copies = [
        pltpu.make_async_copy(
            down_ref.at[j], down_buf.at[pl.ds(j * inner, inner)], down_sems.at[j]
        )
        for j in range(count)
    ]
    for copy in gu_copies + down_copies:
        copy.start()
    for j in range(count):
        gu_copies[j].wait()
        part = jnp.dot(
            x_ref[:, j * depth : (j + 1) * depth], gu_buf[j], preferred_element_type=jnp.float32
        )
        if j == 0:
            act[...] = part
        else:
            act[...] += part
    gate_act, up_act = act[:, :ff], act[:, ff:]
    hidden = (gate_act / (1.0 + jnp.exp(-gate_act)) * up_act).astype(jnp.bfloat16)
    for copy in down_copies:
        copy.wait()
    out_ref[...] = jnp.dot(
        hidden, down_buf[...], preferred_element_type=jnp.float32
    ).astype(jnp.bfloat16)


def expert_mlp(rows, gate_up, down):
    count, depth, both = gate_up.shape
    row_count, width = rows.shape
    inner = down.shape[1]
    return pl.pallas_call(
        mlp_kernel,
        out_shape=jax.ShapeDtypeStruct((row_count, width), jnp.bfloat16),
        in_specs=[pl.BlockSpec(memory_space=pltpu.VMEM)]
        + [pl.BlockSpec(memory_space=pl.ANY)] * 2,
        out_specs=pl.BlockSpec(memory_space=pltpu.VMEM),
        scratch_shapes=[
            pltpu.VMEM((count, depth, both), jnp.bfloat16),
            pltpu.VMEM((count * inner, width), jnp.bfloat16),
            pltpu.VMEM((row_count, both), jnp.float32),
            pltpu.SemaphoreType.DMA((count,)),
            pltpu.SemaphoreType.DMA((count,)),
        ],
        compiler_params=pltpu.CompilerParams(vmem_limit_bytes=48 * 1024 * 1024),
    )(rows, gate_up, down)


def on_device(inputs, route, gain, router, w_gate, w_up, w_down):
    sections = lax.axis_size("section")
    section = lax.axis_index("section")
    micro_count, tok_rows, width = inputs.shape
    top_count = route.shape[-1]
    experts = router.shape[-1]
    capacity = min(2 * tok_rows * top_count // experts, tok_rows)
    slots = experts * capacity
    lanes = 128
    block = capacity * width // lanes

    gate_up = jnp.concatenate([w_gate[0, 0], w_up[0, 0]], axis=1)
    gate_up = gate_up.reshape(sections, width // sections, -1)
    down = w_down[0, 0].reshape(sections, -1, width)
    gate_up_parts = lax.all_to_all(gate_up, "section", 0, 0, tiled=True)
    down_parts = lax.all_to_all(down, "section", 0, 0, tiled=True)

    micro_route = lax.all_to_all(route[0], "section", 0, 0, tiled=True)
    small = jnp.concatenate([router[0], gain[0].reshape(-1, experts)], axis=0)
    small = lax.all_gather(small, "section", axis=0)
    gains = small[:, width:, :].reshape(sections, width).astype(jnp.float32)
    routers = small[:, :width, :]

    expert_ids = jnp.arange(experts, dtype=jnp.int32)
    named = jnp.sum(
        (micro_route[..., None] == expert_ids).astype(jnp.float32), axis=2
    )
    earlier = jnp.tril(jnp.ones((tok_rows, tok_rows), jnp.float32), -1)
    rank = jnp.einsum("ts,lse->lte", earlier, named)
    slot_of = jnp.arange(capacity, dtype=jnp.float32)
    chosen = jnp.where(
        (rank[..., None] == slot_of) & (named[..., None] > 0), 1.0, 0.0
    )
    chosen = chosen.reshape(sections, tok_rows, slots)

    state = lax.dynamic_index_in_dim(inputs, section, 0, keepdims=False)
    outs = []
    for layer in range(sections):
        wide = state.astype(jnp.float32)
        inv_rms = lax.rsqrt(jnp.mean(wide * wide, axis=1, keepdims=True) + EPS)
        normed = (wide * inv_rms * gains[layer]).astype(jnp.bfloat16)
        packed = lax.dot_general(
            chosen[layer].astype(jnp.bfloat16),
            normed,
            (((0,), (0,)), ((), ())),
            preferred_element_type=jnp.float32,
        ).astype(jnp.bfloat16)
        sent = packed.reshape(experts, block, lanes)
        arrived = lax.all_to_all(sent, "dp", 0, 0, tiled=True)
        logits = jnp.dot(normed, routers[layer], preferred_element_type=jnp.float32)
        scores = jax.nn.sigmoid(logits) * named[layer]
        weights = scores / jnp.sum(scores, axis=1, keepdims=True)
        mix = (jnp.repeat(weights, capacity, axis=1)) * chosen[layer]
        mix_high = lax.reduce_precision(mix, 8, 7)
        mix_pair = jnp.concatenate([mix_high, mix - mix_high], axis=0).astype(jnp.bfloat16)

        rows = arrived.reshape(slots, width)
        layer_gu = lax.all_gather(gate_up_parts[layer], "section", axis=0)
        layer_down = lax.all_gather(down_parts[layer], "section", axis=0)
        expert_out = expert_mlp(rows, layer_gu, layer_down)
        returned = lax.all_to_all(
            expert_out.reshape(experts, block, lanes), "dp", 0, 0, tiled=True
        ).reshape(slots, width)
        mixed = jnp.dot(mix_pair, returned, preferred_element_type=jnp.float32)
        state = (wide + (mixed[:tok_rows] + mixed[tok_rows:])).astype(jnp.bfloat16)
        outs.append(state)
    states = lax.all_to_all(jnp.stack(outs), "section", 0, 0, tiled=True)
    return states[None]


def solution(mesh):
    in_specs = (
        P(None, "dp", None),
        P("section", None, "dp", None),
        P("section", None),
        P("section", None, None),
        P("section", "dp", None, None),
        P("section", "dp", None, None),
        P("section", "dp", None, None),
    )
    out_specs = P("section", None, "dp", None)
    return jax.shard_map(
        on_device, mesh=mesh, in_specs=in_specs, out_specs=out_specs, check_vma=False
    )
```

```python
import jax
import jax.numpy as jnp
from jax import lax
from jax.experimental import pallas as pl
from jax.experimental.pallas import tpu as pltpu
from jax.sharding import PartitionSpec as P

EPS = 1e-06
LANES = 128
VMEM_LIMIT = 48 * 1024 * 1024


def normalise(wide, gain_row):
    inv_rms = lax.rsqrt(jnp.mean(wide * wide, axis=1, keepdims=True) + EPS)
    return (wide * inv_rms * gain_row).astype(jnp.bfloat16)


def pack_rows(picker, normed, sent_ref):
    rows = jnp.dot(picker, normed, preferred_element_type=jnp.float32)
    sent_ref[...] = rows.astype(jnp.bfloat16).reshape(sent_ref.shape)


def first_kernel(state_ref, gain_ref, picker_ref, normed_ref, sent_ref):
    normed = normalise(state_ref[...].astype(jnp.float32), gain_ref[...])
    normed_ref[...] = normed
    pack_rows(picker_ref[...], normed, sent_ref)


def mix_rows(returned_ref, mix_ref, state_ref):
    tok_rows, width = state_ref.shape
    rows = returned_ref[...].reshape(returned_ref.shape[0], width)
    mixed = jnp.dot(mix_ref[...], rows, preferred_element_type=jnp.float32)
    total = state_ref[...].astype(jnp.float32) + (mixed[:tok_rows] + mixed[tok_rows:])
    return total.astype(jnp.bfloat16)


def step_kernel(
    returned_ref, mix_ref, state_ref, gain_ref, picker_ref, next_ref, normed_ref, sent_ref
):
    state = mix_rows(returned_ref, mix_ref, state_ref)
    next_ref[...] = state
    normed = normalise(state.astype(jnp.float32), gain_ref[...])
    normed_ref[...] = normed
    pack_rows(picker_ref[...], normed, sent_ref)


def last_kernel(returned_ref, mix_ref, state_ref, next_ref):
    next_ref[...] = mix_rows(returned_ref, mix_ref, state_ref)


def mlp_kernel(split, x_ref, *refs):
    sources = refs[:-4]
    out_ref, held, act, sems = refs[-4:]
    count, depth, both = held.shape
    ff = both // 2
    top = x_ref.shape[1] * x_ref.shape[2] // count
    tall = depth - top
    copies = []
    for part in range(count):
        source = sources[part] if split else sources[0].at[part]
        for place, (start, size) in enumerate(((0, top), (top, tall))):
            copies.append(
                pltpu.make_async_copy(
                    source.at[pl.ds(start, size)],
                    held.at[part, pl.ds(start, size)],
                    sems.at[place, part],
                )
            )
    top_copies, tall_copies = copies[::2], copies[1::2]
    for copy in top_copies + tall_copies:
        copy.start()
    rows = x_ref[...].reshape(x_ref.shape[0], count * top)
    for part in range(count):
        top_copies[part].wait()
        term = jnp.dot(
            rows[:, part * top : (part + 1) * top],
            held[part, :top, :],
            preferred_element_type=jnp.float32,
        )
        if part == 0:
            act[...] = term
        else:
            act[...] += term
    gate_act, up_act = act[:, :ff], act[:, ff:]
    hidden = (gate_act / (1.0 + jnp.exp(-gate_act)) * up_act).astype(jnp.bfloat16)
    outs = []
    for part in range(count):
        tall_copies[part].wait()
        total = None
        for k in range(ff // tall):
            term = jnp.dot(
                hidden[:, k * tall : (k + 1) * tall],
                held[part, top:, k * top : (k + 1) * top],
                preferred_element_type=jnp.float32,
            )
            total = term if total is None else total + term
        outs.append(total.astype(jnp.bfloat16))
    out_ref[...] = jnp.concatenate(outs, axis=1).reshape(out_ref.shape)


def expert_mlp(rows, sources):
    split = len(sources) > 1
    depth, both = sources[0].shape[-2:]
    count = len(sources) if split else sources[0].shape[0]
    return pl.pallas_call(
        lambda *refs: mlp_kernel(split, *refs),
        out_shape=jax.ShapeDtypeStruct(rows.shape, jnp.bfloat16),
        in_specs=[pl.BlockSpec(memory_space=pltpu.VMEM)]
        + [pl.BlockSpec(memory_space=pl.ANY)] * len(sources),
        out_specs=pl.BlockSpec(memory_space=pltpu.VMEM),
        scratch_shapes=[
            pltpu.VMEM((count, depth, both), jnp.bfloat16),
            pltpu.VMEM((rows.shape[0], both), jnp.float32),
            pltpu.SemaphoreType.DMA((2, count)),
        ],
        compiler_params=pltpu.CompilerParams(vmem_limit_bytes=VMEM_LIMIT),
    )(rows, *sources)


def lay_kernel(first_ref, gate_ref, up_ref, down_ref, *out_refs):
    top, ff = gate_ref.shape
    tall = out_refs[0].shape[0] - top
    for place, ref in enumerate(out_refs):

        @pl.when(pl.program_id(0) == place)
        def _(ref=ref):
            ref[:top, :ff] = gate_ref[...]
            ref[:top, ff:] = up_ref[...]
            for k in range(ff // tall):
                ref[top:, k * top : (k + 1) * top] = down_ref[k * tall : (k + 1) * tall, :]


def lay_out(first, gate, up, down, count):
    width, ff = gate.shape
    top = width // count
    depth = top + ff * top // (2 * ff)

    def pick(i, first_ref):
        return lax.rem(first_ref[0] + i, count)

    out = jax.ShapeDtypeStruct((depth, 2 * ff), jnp.bfloat16)
    grid_spec = pltpu.PrefetchScalarGridSpec(
        num_scalar_prefetch=1,
        grid=(count,),
        in_specs=[
            pl.BlockSpec((top, ff), lambda i, first_ref: (pick(i, first_ref), 0)),
            pl.BlockSpec((top, ff), lambda i, first_ref: (pick(i, first_ref), 0)),
            pl.BlockSpec((ff, top), lambda i, first_ref: (0, pick(i, first_ref))),
        ],
        out_specs=[
            pl.BlockSpec((depth, 2 * ff), lambda i, first_ref: (0, 0)) for _ in range(count)
        ],
    )
    return pl.pallas_call(
        lay_kernel,
        grid_spec=grid_spec,
        out_shape=[out] * count,
        compiler_params=pltpu.CompilerParams(vmem_limit_bytes=VMEM_LIMIT),
    )(first.reshape(1).astype(jnp.int32), gate, up, down)


def after(values, *tokens):
    return lax.optimization_barrier((values, tokens))[0]


def on_device(inputs, route, gain, router, w_gate, w_up, w_down):
    sections = lax.axis_size("section")
    section = lax.axis_index("section")
    micro_count, tok_rows, width = inputs.shape
    top_count = route.shape[-1]
    experts = router.shape[-1]
    ff = w_gate.shape[-1]
    capacity = min(2 * tok_rows * top_count // experts, tok_rows)
    slots = experts * capacity
    tiles = width // LANES
    rows_shape = jax.ShapeDtypeStruct((slots, tiles, LANES), jnp.bfloat16)
    tok_shape = jax.ShapeDtypeStruct((tok_rows, width), jnp.bfloat16)
    params = pltpu.CompilerParams(vmem_limit_bytes=VMEM_LIMIT)

    def shifted(part, by):
        return lax.ppermute(
            part, "section", [(i, (i + by) % sections) for i in range(sections)]
        )

    route_values = route[0].reshape(micro_count, -1).astype(jnp.bfloat16)
    route_size = route_values.shape[1]
    padding = -route_size % LANES
    route_values = jnp.pad(route_values, ((0, 0), (0, padding)))
    gain_values = jnp.broadcast_to(gain[0].reshape(1, tiles, LANES), (sections, tiles, LANES))
    brief = jnp.concatenate(
        [gain_values, route_values.reshape(micro_count, -1, LANES)], axis=1
    )
    brief = lax.all_to_all(brief, "section", 0, 0, tiled=True)
    gains = brief[:, :tiles].reshape(sections, 1, width).astype(jnp.float32)
    micro_route = brief[:, tiles:].reshape(sections, -1)[:, :route_size]
    micro_route = micro_route.reshape(sections, tok_rows, top_count).astype(jnp.int32)

    laid = lay_out(section, w_gate[0, 0], w_up[0, 0], w_down[0, 0], sections)
    parts = [laid[0]] + [shifted(laid[by], by) for by in range(1, sections)]

    def own_part(layer, held):
        return lax.select_n(lax.rem(section + sections - layer, sections), *held)

    first_part = own_part(0, parts)
    gathered = [lax.all_gather(first_part, "section", axis=0)]

    dp_count = lax.axis_size("dp")
    core = lax.rem(lax.axis_index("dp"), 2)
    router_half = lax.dynamic_slice_in_dim(router[0], core * (width // 2), width // 2, 0)
    router_half = after(router_half.reshape(-1, LANES), first_part)
    router_halves = [router_half] + [shifted(router_half, by) for by in range(1, sections)]
    own_halves = jnp.stack([own_part(layer, router_halves) for layer in range(sections)])
    other_halves = lax.ppermute(
        own_halves, "dp", [(i, i + 1 - 2 * (i % 2)) for i in range(dp_count)]
    )
    router_pair = jnp.where(core == 0, own_halves, other_halves), jnp.where(
        core == 0, other_halves, own_halves
    )
    routers = jnp.concatenate(router_pair, axis=1).reshape(sections, width, experts)

    expert_ids = jnp.arange(experts, dtype=jnp.int32)
    named = jnp.sum(
        (micro_route[..., None] == expert_ids).astype(jnp.float32), axis=2
    )
    earlier = jnp.tril(jnp.ones((tok_rows, tok_rows), jnp.float32), -1)
    rank = jnp.einsum("ts,lse->lte", earlier, named)
    slot_of = jnp.arange(capacity, dtype=jnp.float32)
    chosen = jnp.where(
        (rank[..., None] == slot_of) & (named[..., None] > 0), 1.0, 0.0
    )
    chosen = chosen.reshape(sections, tok_rows, slots)
    pickers = jnp.swapaxes(chosen, 1, 2).astype(jnp.bfloat16)

    def across(rows):
        blocks = rows.reshape(experts, capacity * tiles, LANES)
        moved = lax.all_to_all(blocks, "dp", 0, 0, tiled=True)
        return moved.reshape(slots, tiles, LANES)

    state = lax.dynamic_index_in_dim(inputs, section, 0, keepdims=False)
    state = after(state, first_part)
    normed, sent = pl.pallas_call(
        first_kernel, out_shape=[tok_shape, rows_shape], compiler_params=params
    )(state, gains[0], pickers[0])
    outs = []
    for layer in range(sections):
        arrived = across(sent)
        logits = jnp.dot(normed, routers[layer], preferred_element_type=jnp.float32)
        scores = jax.nn.sigmoid(logits) * named[layer]
        weights = scores / jnp.sum(scores, axis=1, keepdims=True)
        mix = (jnp.repeat(weights, capacity, axis=1)) * chosen[layer]
        mix_high = lax.reduce_precision(mix, 8, 7)
        mix_pair = jnp.concatenate([mix_high, mix - mix_high], axis=0).astype(jnp.bfloat16)

        if layer == 0:
            held = after(parts, arrived)
            for later in range(1, sections):
                part = own_part(later, held)
                gathered.append(lax.all_gather(part, "section", axis=0))
        expert_out = expert_mlp(arrived, [gathered[layer]])
        returned = across(expert_out)
        if layer + 1 < sections:
            state, normed, sent = pl.pallas_call(
                step_kernel,
                out_shape=[tok_shape, tok_shape, rows_shape],
                compiler_params=params,
            )(returned, mix_pair, state, gains[layer + 1], pickers[layer + 1])
        else:
            state = pl.pallas_call(
                last_kernel, out_shape=tok_shape, compiler_params=params
            )(returned, mix_pair, state)
        outs.append(state)
    states = lax.all_to_all(jnp.stack(outs), "section", 0, 0, tiled=True)
    return states[None]


def solution(mesh):
    in_specs = (
        P(None, "dp", None),
        P("section", None, "dp", None),
        P("section", None),
        P("section", None, None),
        P("section", "dp", None, None),
        P("section", "dp", None, None),
        P("section", "dp", None, None),
    )
    out_specs = P("section", None, "dp", None)
    return jax.shard_map(
        on_device, mesh=mesh, in_specs=in_specs, out_specs=out_specs, check_vma=False
    )
```

```python
import jax
import jax.numpy as jnp
from jax import lax
from jax.experimental import pallas as pl
from jax.experimental.pallas import tpu as pltpu
from jax.sharding import PartitionSpec as P

EPS = 1e-06
LANES = 128
VMEM_LIMIT = 48 * 1024 * 1024


def normalise(wide, gain_row):
    inv_rms = lax.rsqrt(jnp.mean(wide * wide, axis=1, keepdims=True) + EPS)
    return (wide * inv_rms * gain_row).astype(jnp.bfloat16)


def send_rows(rows, out_ref, out_buf, sems):
    half = out_buf.shape[0] // 2
    sends = []
    for block in range(2):
        span = pl.ds(block * half, half)
        part = rows[block * half : (block + 1) * half].astype(jnp.bfloat16)
        out_buf[span] = part.reshape(half, *out_buf.shape[1:])
        send = pltpu.make_async_copy(out_buf.at[span], out_ref.at[span], sems.at[block])
        send.start()
        sends.append(send)
    for send in sends:
        send.wait()


def pack_rows(picker, normed, sent_ref):
    rows = jnp.dot(picker, normed, preferred_element_type=jnp.float32)
    sent_ref[...] = rows.astype(jnp.bfloat16).reshape(sent_ref.shape)


def first_kernel(state_ref, gain_ref, picker_ref, normed_ref, sent_ref):
    normed = normalise(state_ref[...].astype(jnp.float32), gain_ref[...])
    normed_ref[...] = normed
    pack_rows(picker_ref[...], normed, sent_ref)


def mix_rows(returned_ref, mix_ref, state_ref):
    tok_rows, width = state_ref.shape
    rows = returned_ref[...].reshape(returned_ref.shape[0], width)
    mixed = jnp.dot(mix_ref[...], rows, preferred_element_type=jnp.float32)
    total = state_ref[...].astype(jnp.float32) + (mixed[:tok_rows] + mixed[tok_rows:])
    return total.astype(jnp.bfloat16)


def step_kernel(
    returned_ref, mix_ref, state_ref, gain_ref, picker_ref, next_ref, normed_ref, sent_ref
):
    state = mix_rows(returned_ref, mix_ref, state_ref)
    next_ref[...] = state
    normed = normalise(state.astype(jnp.float32), gain_ref[...])
    normed_ref[...] = normed
    pack_rows(picker_ref[...], normed, sent_ref)


def last_kernel(returned_ref, mix_ref, state_ref, next_ref):
    next_ref[...] = mix_rows(returned_ref, mix_ref, state_ref)


def mlp_kernel(split, x_ref, *refs):
    sources = refs[:-6]
    out_ref, held, act, out_buf, sems, out_sems = refs[-6:]
    count, depth, both = held.shape
    ff = both // 2
    top = x_ref.shape[1] * x_ref.shape[2] // count
    tall = depth - top
    copies = []
    for part in range(count):
        source = sources[part] if split else sources[0].at[part]
        for place, (start, size) in enumerate(((0, top), (top, tall))):
            copies.append(
                pltpu.make_async_copy(
                    source.at[pl.ds(start, size)],
                    held.at[part, pl.ds(start, size)],
                    sems.at[place, part],
                )
            )
    top_copies, tall_copies = copies[::2], copies[1::2]
    for copy in top_copies + tall_copies:
        copy.start()
    rows = x_ref[...].reshape(x_ref.shape[0], count * top)
    for part in range(count):
        top_copies[part].wait()
        term = jnp.dot(
            rows[:, part * top : (part + 1) * top],
            held[part, :top, :],
            preferred_element_type=jnp.float32,
        )
        if part == 0:
            act[...] = term
        else:
            act[...] += term
    gate_act, up_act = act[:, :ff], act[:, ff:]
    hidden = (gate_act / (1.0 + jnp.exp(-gate_act)) * up_act).astype(jnp.bfloat16)
    outs = []
    for part in range(count):
        tall_copies[part].wait()
        total = None
        for k in range(ff // tall):
            term = jnp.dot(
                hidden[:, k * tall : (k + 1) * tall],
                held[part, top:, k * top : (k + 1) * top],
                preferred_element_type=jnp.float32,
            )
            total = term if total is None else total + term
        outs.append(total.astype(jnp.bfloat16))
    send_rows(jnp.concatenate(outs, axis=1), out_ref, out_buf, out_sems)


def expert_mlp(rows, sources):
    split = len(sources) > 1
    depth, both = sources[0].shape[-2:]
    count = len(sources) if split else sources[0].shape[0]
    return pl.pallas_call(
        lambda *refs: mlp_kernel(split, *refs),
        out_shape=jax.ShapeDtypeStruct(rows.shape, jnp.bfloat16),
        in_specs=[pl.BlockSpec(memory_space=pltpu.VMEM)]
        + [pl.BlockSpec(memory_space=pl.ANY)] * len(sources),
        out_specs=pl.BlockSpec(memory_space=pltpu.HBM),
        scratch_shapes=[
            pltpu.VMEM((count, depth, both), jnp.bfloat16),
            pltpu.VMEM((rows.shape[0], both), jnp.float32),
            pltpu.VMEM(rows.shape, jnp.bfloat16),
            pltpu.SemaphoreType.DMA((2, count)),
            pltpu.SemaphoreType.DMA((2,)),
        ],
        compiler_params=pltpu.CompilerParams(vmem_limit_bytes=VMEM_LIMIT),
    )(rows, *sources)


def lay_kernel(first_ref, gate_ref, up_ref, down_ref, *out_refs):
    top, ff = gate_ref.shape
    tall = out_refs[0].shape[0] - top
    for place, ref in enumerate(out_refs):

        @pl.when(pl.program_id(0) == place)
        def _(ref=ref):
            ref[:top, :ff] = gate_ref[...]
            ref[:top, ff:] = up_ref[...]
            for k in range(ff // tall):
                ref[top:, k * top : (k + 1) * top] = down_ref[k * tall : (k + 1) * tall, :]


def lay_out(first, gate, up, down, count):
    width, ff = gate.shape
    top = width // count
    depth = top + ff * top // (2 * ff)

    def pick(i, first_ref):
        return lax.rem(first_ref[0] + i, count)

    out = jax.ShapeDtypeStruct((depth, 2 * ff), jnp.bfloat16)
    grid_spec = pltpu.PrefetchScalarGridSpec(
        num_scalar_prefetch=1,
        grid=(count,),
        in_specs=[
            pl.BlockSpec((top, ff), lambda i, first_ref: (pick(i, first_ref), 0)),
            pl.BlockSpec((top, ff), lambda i, first_ref: (pick(i, first_ref), 0)),
            pl.BlockSpec((ff, top), lambda i, first_ref: (0, pick(i, first_ref))),
        ],
        out_specs=[
            pl.BlockSpec((depth, 2 * ff), lambda i, first_ref: (0, 0)) for _ in range(count)
        ],
    )
    return pl.pallas_call(
        lay_kernel,
        grid_spec=grid_spec,
        out_shape=[out] * count,
        compiler_params=pltpu.CompilerParams(vmem_limit_bytes=VMEM_LIMIT),
    )(first.reshape(1).astype(jnp.int32), gate, up, down)


def pick_kernel(which_ref, *refs):
    sources, (out_ref, buf, sems) = refs[:-3], refs[-3:]
    for place, source in enumerate(sources):

        @pl.when(which_ref[0] == place)
        def _(source=source):
            fetch = pltpu.make_async_copy(source, buf, sems.at[0])
            fetch.start()
            fetch.wait()

    send = pltpu.make_async_copy(buf, out_ref, sems.at[1])
    send.start()
    send.wait()


def pick_one(which, arrays):
    return pl.pallas_call(
        pick_kernel,
        out_shape=jax.ShapeDtypeStruct(arrays[0].shape, arrays[0].dtype),
        in_specs=[pl.BlockSpec(memory_space=pltpu.SMEM)]
        + [pl.BlockSpec(memory_space=pl.ANY)] * len(arrays),
        out_specs=pl.BlockSpec(memory_space=pltpu.HBM),
        scratch_shapes=[
            pltpu.VMEM(arrays[0].shape, arrays[0].dtype),
            pltpu.SemaphoreType.DMA((2,)),
        ],
        compiler_params=pltpu.CompilerParams(vmem_limit_bytes=VMEM_LIMIT),
    )(which.reshape(1).astype(jnp.int32), *arrays)


def after(values, *tokens):
    return lax.optimization_barrier((values, tokens))[0]


def on_device(inputs, route, gain, router, w_gate, w_up, w_down):
    sections = lax.axis_size("section")
    section = lax.axis_index("section")
    micro_count, tok_rows, width = inputs.shape
    top_count = route.shape[-1]
    experts = router.shape[-1]
    ff = w_gate.shape[-1]
    capacity = min(2 * tok_rows * top_count // experts, tok_rows)
    slots = experts * capacity
    tiles = width // LANES
    rows_shape = jax.ShapeDtypeStruct((slots, tiles, LANES), jnp.bfloat16)
    tok_shape = jax.ShapeDtypeStruct((tok_rows, width), jnp.bfloat16)
    params = pltpu.CompilerParams(vmem_limit_bytes=VMEM_LIMIT)

    def shifted(part, by):
        return lax.ppermute(
            part, "section", [(i, (i + by) % sections) for i in range(sections)]
        )

    route_values = route[0].reshape(micro_count, -1).astype(jnp.bfloat16)
    route_size = route_values.shape[1]
    padding = -route_size % LANES
    route_values = jnp.pad(route_values, ((0, 0), (0, padding)))
    gain_values = jnp.broadcast_to(gain[0].reshape(1, tiles, LANES), (sections, tiles, LANES))
    brief = jnp.concatenate(
        [gain_values, route_values.reshape(micro_count, -1, LANES)], axis=1
    )
    brief = lax.all_to_all(brief, "section", 0, 0, tiled=True)
    gains = brief[:, :tiles].reshape(sections, 1, width).astype(jnp.float32)
    micro_route = brief[:, tiles:].reshape(sections, -1)[:, :route_size]
    micro_route = micro_route.reshape(sections, tok_rows, top_count).astype(jnp.int32)

    laid = lay_out(section, w_gate[0, 0], w_up[0, 0], w_down[0, 0], sections)
    parts = [laid[0]] + [shifted(laid[by], by) for by in range(1, sections)]

    def own_part(layer, held):
        return lax.select_n(lax.rem(section + sections - layer, sections), *held)

    first_part = pick_one(section, parts)
    gathered = [lax.all_gather(first_part, "section", axis=0)]

    dp_count = lax.axis_size("dp")
    core = lax.rem(lax.axis_index("dp"), 2)
    router_half = lax.dynamic_slice_in_dim(router[0], core * (width // 2), width // 2, 0)
    router_half = after(router_half.reshape(-1, LANES), first_part)
    router_halves = [router_half] + [shifted(router_half, by) for by in range(1, sections)]
    own_halves = jnp.stack([own_part(layer, router_halves) for layer in range(sections)])
    other_halves = lax.ppermute(
        own_halves, "dp", [(i, i + 1 - 2 * (i % 2)) for i in range(dp_count)]
    )
    router_pair = jnp.where(core == 0, own_halves, other_halves), jnp.where(
        core == 0, other_halves, own_halves
    )
    routers = jnp.concatenate(router_pair, axis=1).reshape(sections, width, experts)

    expert_ids = jnp.arange(experts, dtype=jnp.int32)
    named = jnp.sum(
        (micro_route[..., None] == expert_ids).astype(jnp.float32), axis=2
    )
    earlier = jnp.tril(jnp.ones((tok_rows, tok_rows), jnp.float32), -1)
    rank = jnp.einsum("ts,lse->lte", earlier, named)
    slot_of = jnp.arange(capacity, dtype=jnp.float32)
    chosen = jnp.where(
        (rank[..., None] == slot_of) & (named[..., None] > 0), 1.0, 0.0
    )
    chosen = chosen.reshape(sections, tok_rows, slots)
    pickers = jnp.swapaxes(chosen, 1, 2).astype(jnp.bfloat16)

    def across(rows):
        blocks = rows.reshape(experts, capacity * tiles, LANES)
        moved = lax.all_to_all(blocks, "dp", 0, 0, tiled=True)
        return moved.reshape(slots, tiles, LANES)

    state = lax.dynamic_index_in_dim(inputs, section, 0, keepdims=False)
    state = after(state, first_part)
    normed, sent = pl.pallas_call(
        first_kernel,
        out_shape=[tok_shape, rows_shape],
        compiler_params=params,
    )(state, gains[0], pickers[0])
    outs = []
    for layer in range(sections):
        arrived = across(sent)
        logits = jnp.dot(normed, routers[layer], preferred_element_type=jnp.float32)
        scores = jax.nn.sigmoid(logits) * named[layer]
        weights = scores / jnp.sum(scores, axis=1, keepdims=True)
        mix = (jnp.repeat(weights, capacity, axis=1)) * chosen[layer]
        mix_high = lax.reduce_precision(mix, 8, 7)
        mix_pair = jnp.concatenate([mix_high, mix - mix_high], axis=0).astype(jnp.bfloat16)

        if layer == 0:
            held = after(parts, arrived)
            for later in range(1, sections):
                part = own_part(later, held)
                gathered.append(lax.all_gather(part, "section", axis=0))
        expert_out = expert_mlp(arrived, [gathered[layer]])
        if layer + 1 == sections:
            moved = []
            for by in range(1, sections):
                pick = jnp.minimum(lax.rem(section + by, sections), sections - 2)
                moved.append(shifted(lax.select_n(pick, *outs), by))
            expert_out, moved = lax.optimization_barrier((expert_out, moved))
        returned = across(expert_out)
        if layer + 1 < sections:
            state, normed, sent = pl.pallas_call(
                step_kernel,
                out_shape=[tok_shape, tok_shape, rows_shape],
                compiler_params=params,
            )(returned, mix_pair, state, gains[layer + 1], pickers[layer + 1])
        else:
            state = pl.pallas_call(
                last_kernel, out_shape=tok_shape, compiler_params=params
            )(returned, mix_pair, state)
        outs.append(state)
    last = sections - 1
    mine = lax.select_n(section, *outs)
    states = []
    for micro in range(micro_count):
        apart = lax.rem(section + sections - micro, sections)
        home = lax.select_n(apart, mine, *moved)
        if micro != last:
            final = lax.ppermute(outs[last], "section", [(micro, last)])
            home = jnp.where(section == last, final, home)
        states.append(home)
    return jnp.stack(states)[None]


def solution(mesh):
    in_specs = (
        P(None, "dp", None),
        P("section", None, "dp", None),
        P("section", None),
        P("section", None, None),
        P("section", "dp", None, None),
        P("section", "dp", None, None),
        P("section", "dp", None, None),
    )
    out_specs = P("section", None, "dp", None)
    return jax.shard_map(
        on_device, mesh=mesh, in_specs=in_specs, out_specs=out_specs, check_vma=False
    )
```

```python
import jax
import jax.numpy as jnp
from jax import lax
from jax.experimental import pallas as pl
from jax.experimental.pallas import tpu as pltpu
from jax.sharding import PartitionSpec as P

EPS = 1e-06
LANES = 128
VMEM_LIMIT = 48 * 1024 * 1024


def normalise(wide, gain_row):
    inv_rms = lax.rsqrt(jnp.mean(wide * wide, axis=1, keepdims=True) + EPS)
    return (wide * inv_rms * gain_row).astype(jnp.bfloat16)


def send_rows(rows, out_ref, out_buf, sems):
    half = out_buf.shape[0] // 2
    sends = []
    for block in range(2):
        span = pl.ds(block * half, half)
        part = rows[block * half : (block + 1) * half].astype(jnp.bfloat16)
        out_buf[span] = part.reshape(half, *out_buf.shape[1:])
        send = pltpu.make_async_copy(out_buf.at[span], out_ref.at[span], sems.at[block])
        send.start()
        sends.append(send)
    for send in sends:
        send.wait()


def pack_rows(picker, normed, sent_ref):
    rows = jnp.dot(picker, normed, preferred_element_type=jnp.float32)
    sent_ref[...] = rows.astype(jnp.bfloat16).reshape(sent_ref.shape)


def first_kernel(state_ref, gain_ref, picker_ref, normed_ref, sent_ref):
    normed = normalise(state_ref[...].astype(jnp.float32), gain_ref[...])
    normed_ref[...] = normed
    pack_rows(picker_ref[...], normed, sent_ref)


def mix_rows(returned_ref, mix_ref, state_ref):
    tok_rows, width = state_ref.shape
    rows = returned_ref[...].reshape(returned_ref.shape[0], width)
    mixed = jnp.dot(mix_ref[...], rows, preferred_element_type=jnp.float32)
    total = state_ref[...].astype(jnp.float32) + (mixed[:tok_rows] + mixed[tok_rows:])
    return total.astype(jnp.bfloat16)


def step_kernel(
    returned_ref, mix_ref, state_ref, gain_ref, picker_ref, next_ref, normed_ref, sent_ref
):
    state = mix_rows(returned_ref, mix_ref, state_ref)
    next_ref[...] = state
    normed = normalise(state.astype(jnp.float32), gain_ref[...])
    normed_ref[...] = normed
    pack_rows(picker_ref[...], normed, sent_ref)


def last_kernel(returned_ref, mix_ref, state_ref, next_ref):
    next_ref[...] = mix_rows(returned_ref, mix_ref, state_ref)


def mlp_kernel(split, x_ref, *refs):
    sources = refs[:-6]
    out_ref, held, act, out_buf, sems, out_sems = refs[-6:]
    count, depth, both = held.shape
    ff = both // 2
    top = x_ref.shape[1] * x_ref.shape[2] // count
    tall = depth - top
    copies = []
    for part in range(count):
        source = sources[part] if split else sources[0].at[part]
        for place, (start, size) in enumerate(((0, top), (top, tall))):
            copies.append(
                pltpu.make_async_copy(
                    source.at[pl.ds(start, size)],
                    held.at[part, pl.ds(start, size)],
                    sems.at[place, part],
                )
            )
    top_copies, tall_copies = copies[::2], copies[1::2]
    for copy in top_copies + tall_copies:
        copy.start()
    rows = x_ref[...].reshape(x_ref.shape[0], count * top)
    for part in range(count):
        top_copies[part].wait()
        term = jnp.dot(
            rows[:, part * top : (part + 1) * top],
            held[part, :top, :],
            preferred_element_type=jnp.float32,
        )
        if part == 0:
            act[...] = term
        else:
            act[...] += term
    gate_act, up_act = act[:, :ff], act[:, ff:]
    hidden = (gate_act / (1.0 + jnp.exp(-gate_act)) * up_act).astype(jnp.bfloat16)
    outs = []
    for part in range(count):
        tall_copies[part].wait()
        total = None
        for k in range(ff // tall):
            term = jnp.dot(
                hidden[:, k * tall : (k + 1) * tall],
                held[part, top:, k * top : (k + 1) * top],
                preferred_element_type=jnp.float32,
            )
            total = term if total is None else total + term
        outs.append(total.astype(jnp.bfloat16))
    send_rows(jnp.concatenate(outs, axis=1), out_ref, out_buf, out_sems)


def expert_mlp(rows, sources):
    split = len(sources) > 1
    depth, both = sources[0].shape[-2:]
    count = len(sources) if split else sources[0].shape[0]
    return pl.pallas_call(
        lambda *refs: mlp_kernel(split, *refs),
        out_shape=jax.ShapeDtypeStruct(rows.shape, jnp.bfloat16),
        in_specs=[pl.BlockSpec(memory_space=pltpu.VMEM)]
        + [pl.BlockSpec(memory_space=pl.ANY)] * len(sources),
        out_specs=pl.BlockSpec(memory_space=pltpu.HBM),
        scratch_shapes=[
            pltpu.VMEM((count, depth, both), jnp.bfloat16),
            pltpu.VMEM((rows.shape[0], both), jnp.float32),
            pltpu.VMEM(rows.shape, jnp.bfloat16),
            pltpu.SemaphoreType.DMA((2, count)),
            pltpu.SemaphoreType.DMA((2,)),
        ],
        compiler_params=pltpu.CompilerParams(vmem_limit_bytes=VMEM_LIMIT),
    )(rows, *sources)


def lay_kernel(first_ref, gate_ref, up_ref, down_ref, *out_refs):
    top, ff = gate_ref.shape
    tall = out_refs[0].shape[0] - top
    for place, ref in enumerate(out_refs):

        @pl.when(pl.program_id(0) == place)
        def _(ref=ref):
            ref[:top, :ff] = gate_ref[...]
            ref[:top, ff:] = up_ref[...]
            for k in range(ff // tall):
                ref[top:, k * top : (k + 1) * top] = down_ref[k * tall : (k + 1) * tall, :]


def lay_out(first, gate, up, down, count):
    width, ff = gate.shape
    top = width // count
    depth = top + ff * top // (2 * ff)

    def pick(i, first_ref):
        return lax.rem(first_ref[0] + i, count)

    out = jax.ShapeDtypeStruct((depth, 2 * ff), jnp.bfloat16)
    grid_spec = pltpu.PrefetchScalarGridSpec(
        num_scalar_prefetch=1,
        grid=(count,),
        in_specs=[
            pl.BlockSpec((top, ff), lambda i, first_ref: (pick(i, first_ref), 0)),
            pl.BlockSpec((top, ff), lambda i, first_ref: (pick(i, first_ref), 0)),
            pl.BlockSpec((ff, top), lambda i, first_ref: (0, pick(i, first_ref))),
        ],
        out_specs=[
            pl.BlockSpec((depth, 2 * ff), lambda i, first_ref: (0, 0)) for _ in range(count)
        ],
    )
    return pl.pallas_call(
        lay_kernel,
        grid_spec=grid_spec,
        out_shape=[out] * count,
        compiler_params=pltpu.CompilerParams(vmem_limit_bytes=VMEM_LIMIT),
    )(first.reshape(1).astype(jnp.int32), gate, up, down)


def pick_kernel(which_ref, *refs):
    sources, (out_ref, buf, sems) = refs[:-3], refs[-3:]
    for place, source in enumerate(sources):

        @pl.when(which_ref[0] == place)
        def _(source=source):
            fetch = pltpu.make_async_copy(source, buf, sems.at[0])
            fetch.start()
            fetch.wait()

    send = pltpu.make_async_copy(buf, out_ref, sems.at[1])
    send.start()
    send.wait()


def pick_one(which, arrays):
    return pl.pallas_call(
        pick_kernel,
        out_shape=jax.ShapeDtypeStruct(arrays[0].shape, arrays[0].dtype),
        in_specs=[pl.BlockSpec(memory_space=pltpu.SMEM)]
        + [pl.BlockSpec(memory_space=pl.ANY)] * len(arrays),
        out_specs=pl.BlockSpec(memory_space=pltpu.HBM),
        scratch_shapes=[
            pltpu.VMEM(arrays[0].shape, arrays[0].dtype),
            pltpu.SemaphoreType.DMA((2,)),
        ],
        compiler_params=pltpu.CompilerParams(vmem_limit_bytes=VMEM_LIMIT),
    )(which.reshape(1).astype(jnp.int32), *arrays)


def after(values, *tokens):
    return lax.optimization_barrier((values, tokens))[0]


def on_device(inputs, route, gain, router, w_gate, w_up, w_down):
    sections = lax.axis_size("section")
    section = lax.axis_index("section")
    micro_count, tok_rows, width = inputs.shape
    top_count = route.shape[-1]
    experts = router.shape[-1]
    ff = w_gate.shape[-1]
    capacity = min(2 * tok_rows * top_count // experts, tok_rows)
    slots = experts * capacity
    tiles = width // LANES
    rows_shape = jax.ShapeDtypeStruct((slots, tiles, LANES), jnp.bfloat16)
    tok_shape = jax.ShapeDtypeStruct((tok_rows, width), jnp.bfloat16)
    params = pltpu.CompilerParams(vmem_limit_bytes=VMEM_LIMIT)

    def shifted(part, by):
        return lax.ppermute(
            part, "section", [(i, (i + by) % sections) for i in range(sections)]
        )

    route_values = route[0].reshape(micro_count, -1).astype(jnp.bfloat16)
    route_size = route_values.shape[1]
    padding = -route_size % LANES
    route_values = jnp.pad(route_values, ((0, 0), (0, padding)))
    gain_values = jnp.broadcast_to(gain[0].reshape(1, tiles, LANES), (sections, tiles, LANES))
    brief = jnp.concatenate(
        [gain_values, route_values.reshape(micro_count, -1, LANES)], axis=1
    )
    brief = lax.all_to_all(brief, "section", 0, 0, tiled=True)
    gains = brief[:, :tiles].reshape(sections, 1, width).astype(jnp.float32)
    micro_route = brief[:, tiles:].reshape(sections, -1)[:, :route_size]
    micro_route = micro_route.reshape(sections, tok_rows, top_count).astype(jnp.int32)

    laid = lay_out(section, w_gate[0, 0], w_up[0, 0], w_down[0, 0], sections)
    parts = [laid[0]] + [shifted(laid[by], by) for by in range(1, sections)]

    def own_part(layer, held):
        return lax.select_n(lax.rem(section + sections - layer, sections), *held)

    first_part = pick_one(section, parts)
    gathered = [lax.all_gather(first_part, "section", axis=0)]

    dp_count = lax.axis_size("dp")
    core = lax.rem(lax.axis_index("dp"), 2)
    router_half = lax.dynamic_slice_in_dim(router[0], core * (width // 2), width // 2, 0)
    router_half = after(router_half.reshape(-1, LANES), first_part)
    router_halves = [router_half] + [shifted(router_half, by) for by in range(1, sections)]
    own_halves = jnp.stack([own_part(layer, router_halves) for layer in range(sections)])
    other_halves = lax.ppermute(
        own_halves, "dp", [(i, i + 1 - 2 * (i % 2)) for i in range(dp_count)]
    )
    router_pair = jnp.where(core == 0, own_halves, other_halves), jnp.where(
        core == 0, other_halves, own_halves
    )
    routers = jnp.concatenate(router_pair, axis=1).reshape(sections, width, experts)

    expert_ids = jnp.arange(experts, dtype=jnp.int32)
    named = jnp.sum(
        (micro_route[..., None] == expert_ids).astype(jnp.float32), axis=2
    )
    earlier = jnp.tril(jnp.ones((tok_rows, tok_rows), jnp.float32), -1)
    rank = jnp.einsum("ts,lse->lte", earlier, named)
    slot_of = jnp.arange(capacity, dtype=jnp.float32)
    chosen = jnp.where(
        (rank[..., None] == slot_of) & (named[..., None] > 0), 1.0, 0.0
    )
    chosen = chosen.reshape(sections, tok_rows, slots)
    pickers = jnp.swapaxes(chosen, 1, 2).astype(jnp.bfloat16)

    def across(rows):
        blocks = rows.reshape(experts, capacity * tiles, LANES)
        moved = lax.all_to_all(blocks, "dp", 0, 0, tiled=True)
        return moved.reshape(slots, tiles, LANES)

    state = lax.dynamic_index_in_dim(inputs, section, 0, keepdims=False)
    state = after(state, first_part)
    normed, sent = pl.pallas_call(
        first_kernel,
        out_shape=[tok_shape, rows_shape],
        compiler_params=params,
    )(state, gains[0], pickers[0])
    outs = []
    for layer in range(sections):
        arrived = across(sent)
        logits = jnp.dot(normed, routers[layer], preferred_element_type=jnp.float32)
        scores = jax.nn.sigmoid(logits) * named[layer]
        weights = scores / jnp.sum(scores, axis=1, keepdims=True)
        mix = (jnp.repeat(weights, capacity, axis=1)) * chosen[layer]
        mix_high = lax.reduce_precision(mix, 8, 7)
        mix_pair = jnp.concatenate([mix_high, mix - mix_high], axis=0).astype(jnp.bfloat16)

        if layer == 0:
            held = after(parts, arrived)
            for later in range(1, sections):
                part = own_part(later, held)
                gathered.append(lax.all_gather(part, "section", axis=0))
        expert_out = expert_mlp(arrived, [gathered[layer]])
        returned = across(expert_out)
        if layer + 1 < sections:
            state, normed, sent = pl.pallas_call(
                step_kernel,
                out_shape=[tok_shape, tok_shape, rows_shape],
                compiler_params=params,
            )(returned, mix_pair, state, gains[layer + 1], pickers[layer + 1])
        else:
            state = pl.pallas_call(
                last_kernel, out_shape=tok_shape, compiler_params=params
            )(returned, mix_pair, state)
        outs.append(state)
    states = lax.all_to_all(jnp.stack(outs), "section", 0, 0, tiled=True)
    return states[None]


def solution(mesh):
    in_specs = (
        P(None, "dp", None),
        P("section", None, "dp", None),
        P("section", None),
        P("section", None, None),
        P("section", "dp", None, None),
        P("section", "dp", None, None),
        P("section", "dp", None, None),
    )
    out_specs = P("section", None, "dp", None)
    return jax.shard_map(
        on_device, mesh=mesh, in_specs=in_specs, out_specs=out_specs, check_vma=False
    )
```
